32 devices in a mesh: dp: 16 (over z, y, x), rep: 2 (over core).
Axes of the slice: x: 2, y: 2, z: 4, core: 2. Of those that a mesh axis runs over, the one named last changes fastest.
Arguments:
- queries: bfloat16 [32768, 1024], P(('dp', 'rep')), may hold values from -12 to 12
- keys: bfloat16 [2048, 1024], P('dp'), may hold values from -5 to 5
- neg_mask: int32 [256, 16], P(('dp', 'rep')), may hold values from 0 to 1, as said below
- positive: int32 [256], P(('dp', 'rep')), may hold values from 0 to 15, as said below
- row_weight: float32 [32768], P(('dp', 'rep')), may hold values from 2 to 20
Outputs:
- row_loss: float32 [32768], P(('dp', 'rep'))
- grad_queries: float32 [32768, 1024], P(('dp', 'rep'))
- grad_keys: float32 [2048, 1024], P(('dp', 'rep'))
The draws below stay inside these ranges and needn't reach their ends.
Inputs may be any that keep to these rules, and one draw needn't show every extreme that they name: neg_mask[b, c] is 0 unless key block c lies at cyclic distance at most 4 from the dp index that holds query block b (query blocks numbered along dp+rep, 8 to a device); for every b the two key blocks at distance exactly 4 are 1. positive[b] lies at cyclic distance at most 4 from the dp index that holds query block b.
All inputs are finite; a program needn't handle non-finite values.
Results may differ from the reference program's by a relative error of at most 0.003.
Values may be sent and summed in bfloat16 or wider, within the bound.
A program may use at most 128 MiB of HBM per device.

```python
import math
import jax
import jax.numpy as jnp
from jax import lax

D = 1024
BLOCK = 128
REACH = 4
QB_DEV = 8
NQB = 256
NKB = 16
NQ = 32768
NK = 2048
N_DP = 16
N_REP = 2


def positive_blocks(key):
    block_ids = jnp.arange(NQB, dtype=jnp.int32)
    home_idx = block_ids // (QB_DEV * N_REP)
    offset_draw = jax.random.randint(jax.random.fold_in(key, 7), (NQB,), -REACH, REACH + 1, dtype=jnp.int32)
    target = (home_idx + offset_draw) % N_DP
    target = jnp.where(block_ids == 0, N_DP - 1, target)
    target = jnp.where(block_ids == NQB - 1, 0, target)
    return target.astype(jnp.int32)


def key_table(key):
    key_base = jax.random.fold_in(key, 11)
    return jnp.clip(jax.random.normal(key_base, (NK, D), jnp.float32), -4.5, 4.5)


def draw_keys(key, part):
    return key_table(key).astype(jnp.bfloat16)


def draw_positive(key, part):
    return positive_blocks(key)


def draw_queries(key, part):
    table = key_table(key)
    target = positive_blocks(key)
    row_ids = jnp.arange(NQ, dtype=jnp.int32)
    block_ids = row_ids // BLOCK
    key_rows = target[block_ids] * BLOCK + row_ids % BLOCK
    positive_keys = table[key_rows]
    noise_key = jax.random.fold_in(key, 17)
    noise_part = jnp.clip(jax.random.normal(noise_key, (NQ, D), jnp.float32), -4.5, 4.5)
    mixed = 0.1 * positive_keys + noise_part
    return mixed.astype(jnp.bfloat16)


def draw_neg_mask(key, part):
    key_one = jax.random.fold_in(key, 13)
    key_two = jax.random.fold_in(key, 23)
    block_ids = jnp.arange(NQB, dtype=jnp.int32)
    home_idx = block_ids // (QB_DEV * N_REP)
    key_blocks = jnp.arange(NKB, dtype=jnp.int32)
    distance = (key_blocks[None, :] - home_idx[:, None]) % N_DP
    nearby = (distance <= REACH) | (distance >= N_DP - REACH)
    density = jax.random.randint(key_one, (NQB, 1), 1, 9, dtype=jnp.int32)
    coin_draw = jax.random.randint(key_two, (NQB, NKB), 0, 8, dtype=jnp.int32)
    chosen = nearby & (coin_draw < density)
    boundary = (distance == REACH) | (distance == N_DP - REACH)
    return jnp.where(chosen | boundary, 1, 0).astype(jnp.int32)


def block_scale(own_key, shape, split, low, largest):
    def one(dim, shards_of):
        draws = jax.random.uniform(jax.random.fold_in(jax.random.fold_in(own_key, 6), dim), (shards_of,), jnp.float32, low / len(split), largest / len(split))
        return jnp.repeat(jnp.exp(draws), shape[dim] // shards_of).reshape((-1,) + (1,) * (len(shape) - dim - 1))

    factor_of = one(*split[0])
    for cut in split[1:]:
        factor_of = factor_of * one(*cut)
    return factor_of


def setup_inputs(seed: int = 0) -> dict:
    splits = jax.random.split(jax.random.key(seed), 6)
    return {
        "queries": draw_queries(jax.random.fold_in(splits[5], 71), 0),
        "keys": draw_keys(jax.random.fold_in(splits[5], 71), 0),
        "neg_mask": draw_neg_mask(jax.random.fold_in(splits[5], 71), 0),
        "positive": draw_positive(jax.random.fold_in(splits[5], 71), 0),
        "row_weight": jnp.clip(jnp.exp(math.log(20.0) - 2.3025851 * jax.random.uniform(splits[4], (NQ,), jnp.float32) ** block_scale(splits[4], (NQ,), ((0, 32),), -0.2, 0.2)), 2.0, 20.0),
    }


def reference(queries, keys, neg_mask, positive, row_weight):
    logit_scale = 2.0 / math.sqrt(D)
    block_count = N_REP * QB_DEV
    group_rows = block_count * BLOCK
    window_len = 2 * REACH + 1
    offsets = jnp.arange(-REACH, REACH + 1, dtype=jnp.int32)
    inner_idx = jnp.arange(BLOCK, dtype=jnp.int32)
    same_row = inner_idx[:, None] == inner_idx[None, :]

    def one_shard(grad_keys, home_idx):
        first_block = (home_idx * block_count).astype(jnp.int32)
        first_row = (first_block * BLOCK).astype(jnp.int32)
        query_rows = lax.dynamic_slice_in_dim(queries, first_row, group_rows, 0)
        weights = lax.dynamic_slice_in_dim(row_weight, first_row, group_rows, 0)
        blocks = lax.dynamic_slice_in_dim(neg_mask, first_block, block_count, 0)
        pos_blocks = lax.dynamic_slice_in_dim(positive, first_block, block_count, 0)
        window = ((home_idx + offsets) % N_DP).astype(jnp.int32)
        key_rows = (window[:, None] * BLOCK + inner_idx[None, :]).reshape(window_len * BLOCK).astype(jnp.int32)
        window_keys = jnp.take(keys, key_rows, axis=0)
        logits = logit_scale * jnp.dot(query_rows, window_keys.T, preferred_element_type=jnp.float32)
        hit_block = pos_blocks[:, None] == window[None, :]
        allow_block = (jnp.take(blocks, window, axis=1) == 1) | hit_block
        allowed = jnp.broadcast_to(allow_block[:, None, :, None], (block_count, BLOCK, window_len, BLOCK)).reshape(group_rows, window_len * BLOCK)
        at_positive = (hit_block[:, None, :, None] & same_row[None, :, None, :]).reshape(group_rows, window_len * BLOCK)
        masked = jnp.where(allowed, logits, jnp.float32(-1e+30))
        row_max = lax.optimization_barrier(jnp.max(masked, axis=1, keepdims=True))
        row_sum = lax.optimization_barrier(jnp.sum(jnp.exp(masked - row_max), axis=1, keepdims=True))
        log_total = row_max + jnp.log(row_sum)
        pos_logit = lax.optimization_barrier(jnp.sum(jnp.where(at_positive, logits, jnp.float32(0.0)), axis=1))
        row_losses = log_total[:, 0] - pos_logit
        softmax_p = jnp.exp(masked - log_total)
        coefficient = (weights[:, None] * (softmax_p - at_positive.astype(jnp.float32))).astype(jnp.bfloat16)
        grad_query = logit_scale * jnp.dot(coefficient, window_keys, preferred_element_type=jnp.float32)
        grad_part = logit_scale * jnp.dot(coefficient.T, query_rows, preferred_element_type=jnp.float32)
        grad_keys = grad_keys.at[key_rows].add(grad_part)
        return (grad_keys, (row_losses, grad_query))
    grad_keys, outputs = lax.scan(one_shard, jnp.zeros((NK, D), jnp.float32), jnp.arange(N_DP, dtype=jnp.int32))
    row_losses, grad_query = outputs
    return (row_losses.reshape(NQ), grad_query.reshape(NQ, D), grad_keys)
```

```python
import functools
import math

import jax
import jax.numpy as jnp
from jax import lax
from jax.experimental import pallas as pl
from jax.experimental.pallas import tpu as pltpu
from jax.sharding import PartitionSpec as P

REACH = 4
NEG = -1e30


def kernel(n, q_hbm, k_hbm, mask, positive, weight, loss, gq_hbm, gk_out,
           q, kwin, e, coef, gk, sib, outb, inb, gq, run_max, run_sum, pos_logit, hist,
           local_sem, g_send, g_recv, f_send, f_recv, x_send, x_recv, s_send, s_recv, o_sem):
    rows, width = q.shape
    blocks, tile = weight.shape
    half = tile // 2
    scale = 2.0 / math.sqrt(width)
    d = lax.axis_index("dp")
    r = lax.axis_index("rep")
    other = 1 - r

    def dev(by):
        return lax.rem(d + by + n, n)

    def owner_of(p):
        j = (p + 1) // 2
        return dev(jnp.where(p % 2 == 1, j, -j) if not isinstance(p, int) else (j if p % 2 else -j))

    q_copy = pltpu.make_async_copy(q_hbm, q, local_sem.at[0])
    q_copy.start()
    own = [
        pltpu.make_async_copy(k_hbm.at[pl.ds(h * half, half)], kwin.at[0, h], local_sem.at[1 + h])
        for h in range(2)
    ]
    for c in own:
        c.start()

    barrier = pltpu.get_barrier_semaphore()
    for by in range(1, REACH + 1):
        for sign in (1, -1):
            pl.semaphore_signal(barrier, inc=1, device_id={"dp": dev(sign * by)},
                                device_id_type=pl.DeviceIdType.MESH)
    pl.semaphore_signal(barrier, inc=1, device_id={"rep": other},
                        device_id_type=pl.DeviceIdType.MESH)
    pl.semaphore_wait(barrier, 2 * REACH + 1)

    def gather(p_dst, by):
        return pltpu.make_async_remote_copy(
            src_ref=k_hbm.at[pl.ds(pl.multiple_of(r * half, half), half)],
            dst_ref=kwin.at[p_dst, r],
            send_sem=g_send.at[p_dst], recv_sem=g_recv.at[p_dst],
            device_id={"dp": dev(by)}, device_id_type=pl.DeviceIdType.MESH)

    def forward(p, h):
        return pltpu.make_async_remote_copy(
            src_ref=kwin.at[p, h], dst_ref=kwin.at[p, h],
            send_sem=f_send.at[p], recv_sem=f_recv.at[p],
            device_id={"rep": other}, device_id_type=pl.DeviceIdType.MESH)

    for j in range(1, REACH + 1):
        gather(2 * j, j).start()
        gather(2 * j - 1, -j).start()

    run_max[...] = jnp.full(run_max.shape, NEG, jnp.float32)
    run_sum[...] = jnp.zeros(run_sum.shape, jnp.float32)
    pos_logit[...] = jnp.zeros(pos_logit.shape, jnp.float32)
    eye = (lax.broadcasted_iota(jnp.int32, (tile, tile), 0)
           == lax.broadcasted_iota(jnp.int32, (tile, tile), 1))
    eye_f = eye.astype(jnp.float32)

    def chunk(j, owners, first, count):
        k = kwin[pl.ds(first, count)].reshape(count * tile, width)
        group = 2 if blocks % 2 == 0 else 1
        for g in range(blocks // group):
            logit = lax.dot_general(
                k, q[g * group * tile:(g + 1) * group * tile, :],
                (((1,), (1,)), ((), ())), preferred_element_type=jnp.float32)
            for bb in range(group):
                b = g * group + bb
                lanes = slice(bb * tile, (bb + 1) * tile)
                old = run_max[b:b + 1, :]
                top = old
                masked = []
                found = pos_logit[b:b + 1, :]
                for i in range(count):
                    part = logit[i * tile:(i + 1) * tile, lanes] * scale
                    hit = positive[b] == owners[i]
                    allow = (mask[b, owners[i]] == 1) | hit
                    found = found + jnp.where(hit, 1.0, 0.0) * jnp.sum(
                        jnp.where(eye, part, 0.0), axis=0, keepdims=True)
                    part = part + jnp.where(allow, 0.0, NEG)
                    masked.append(part)
                    top = jnp.maximum(top, jnp.max(part, axis=0, keepdims=True))
                total = run_sum[b:b + 1, :] * jnp.exp(old - top)
                for i in range(count):
                    ex = jnp.exp(masked[i] - top)
                    total = total + jnp.sum(ex, axis=0, keepdims=True)
                    e[first + i, :, b * tile:(b + 1) * tile] = ex
                run_max[b:b + 1, :] = top
                run_sum[b:b + 1, :] = total
                pos_logit[b:b + 1, :] = found
        hist[j] = run_max[...]

    q_copy.wait()
    for c in own:
        c.wait()
    chunk(0, [d], 0, 1)

    @pl.loop(1, REACH + 1)
    def _(j):
        for p in (2 * j - 1, 2 * j):
            gather(p, 0).wait_recv()
            forward(p, r).start()
        for p in (2 * j - 1, 2 * j):
            forward(p, other).wait_recv()
        chunk(j, [dev(j), dev(-j)], 2 * j - 1, 2)

    log_total = run_max[...] + jnp.log(run_sum[...])
    loss[...] = log_total - pos_logit[...]
    w_over = weight[...] / run_sum[...]

    def finish(j, owners, first):
        factor = w_over * jnp.exp(hist[j] - run_max[...])
        for b in range(blocks):
            lanes = slice(b * tile, (b + 1) * tile)
            for i, owner in enumerate(owners):
                at = jnp.where(positive[b] == owner, 1.0, 0.0) * weight[b:b + 1, :]
                coef[first + i, :, lanes] = (
                    e[first + i, :, lanes] * factor[b:b + 1, :] - at * eye_f
                ).astype(jnp.bfloat16)

    def exchange(p, h):
        return pltpu.make_async_remote_copy(
            src_ref=gk.at[p, h], dst_ref=sib.at[p],
            send_sem=x_send.at[p], recv_sem=x_recv.at[p],
            device_id={"rep": other}, device_id_type=pl.DeviceIdType.MESH)

    def scatter(p, p_dst, to):
        return pltpu.make_async_remote_copy(
            src_ref=outb.at[p], dst_ref=inb.at[p_dst],
            send_sem=s_send.at[p], recv_sem=s_recv.at[p_dst],
            device_id={"dp": to}, device_id_type=pl.DeviceIdType.MESH)

    def key_grad(first, count):
        c = coef[pl.ds(first, count)].reshape(count * tile, rows)
        for g in range(4):
            cols = slice(g * (width // 4), (g + 1) * (width // 4))
            part = scale * jnp.dot(c, q[:, cols], preferred_element_type=jnp.float32)
            gk[pl.ds(first, count), :, :, cols] = part.reshape(count, 2, half, width // 4)

    def ship(j):
        for p, p_dst, by in ((2 * j - 1, 2 * j, j), (2 * j, 2 * j - 1, -j)):
            exchange(p, other).wait_recv()
            outb[p] = (gk[p, r] + sib[p]).astype(jnp.bfloat16)
            scatter(p, p_dst, dev(by)).start()

    @pl.loop(0, REACH)
    def _(i):
        j = REACH - i
        finish(j, [dev(j), dev(-j)], 2 * j - 1)
        key_grad(2 * j - 1, 2)
        for p in (2 * j - 1, 2 * j):
            exchange(p, other).start()

        @pl.when(i > 0)
        def _():
            ship(j + 1)

    finish(0, [d], 0)
    key_grad(0, 1)
    exchange(0, other).start()
    ship(1)

    k_all = kwin[...].reshape((2 * REACH + 1) * tile, width)
    c_all = coef
    step = rows // 4
    for g in range(4):
        ct = c_all[:, :, g * step:(g + 1) * step].reshape((2 * REACH + 1) * tile, step)
        gq[g * step:(g + 1) * step, :] = scale * lax.dot_general(
            ct, k_all, (((0,), (0,)), ((), ())), preferred_element_type=jnp.float32)
        pltpu.make_async_copy(gq.at[pl.ds(g * step, step)], gq_hbm.at[pl.ds(g * step, step)],
                              o_sem.at[g]).start()

    exchange(0, other).wait_recv()
    acc = gk[0, r] + sib[0]
    for p in range(1, 2 * REACH + 1):
        scatter(p, p, d).wait_recv()
        acc = acc + inb[p].astype(jnp.float32)
    gk_out[...] = acc

    for g in range(4):
        pltpu.make_async_copy(gq.at[pl.ds(g * step, step)], gq_hbm.at[pl.ds(g * step, step)],
                              o_sem.at[g]).wait()
    exchange(0, other).wait_send()
    for p in range(1, 2 * REACH + 1):
        gather(p, 0).wait_send()
        forward(p, r).wait_send()
        exchange(p, other).wait_send()
        scatter(p, p, d).wait_send()


def body(queries, keys, neg_mask, positive, row_weight):
    n = lax.axis_size("dp")
    rows, width = queries.shape
    tile = keys.shape[0]
    blocks = rows // tile
    half = tile // 2
    slots = 2 * REACH + 1
    any_, vmem, smem = (pl.BlockSpec(memory_space=m) for m in (pl.ANY, pltpu.VMEM, pltpu.SMEM))
    f32, bf16 = jnp.float32, jnp.bfloat16
    dma = pltpu.SemaphoreType.DMA
    loss, gq, gk = pl.pallas_call(
        functools.partial(kernel, n),
        out_shape=(
            jax.ShapeDtypeStruct((blocks, tile), f32),
            jax.ShapeDtypeStruct((rows, width), f32),
            jax.ShapeDtypeStruct((half, width), f32),
        ),
        in_specs=[any_, any_, smem, smem, vmem],
        out_specs=(vmem, any_, vmem),
        scratch_shapes=[
            pltpu.VMEM((rows, width), bf16),
            pltpu.VMEM((slots, 2, half, width), bf16),
            pltpu.VMEM((slots, tile, rows), f32),
            pltpu.VMEM((slots, tile, rows), bf16),
            pltpu.VMEM((slots, 2, half, width), f32),
            pltpu.VMEM((slots, half, width), f32),
            pltpu.VMEM((slots, half, width), bf16),
            pltpu.VMEM((slots, half, width), bf16),
            pltpu.VMEM((rows, width), f32),
            pltpu.VMEM((blocks, tile), f32),
            pltpu.VMEM((blocks, tile), f32),
            pltpu.VMEM((blocks, tile), f32),
            pltpu.VMEM((REACH + 1, blocks, tile), f32),
            dma((3,)),
            dma((slots,)), dma((slots,)), dma((slots,)), dma((slots,)),
            dma((slots,)), dma((slots,)), dma((slots,)), dma((slots,)),
            dma((4,)),
        ],
        compiler_params=pltpu.CompilerParams(
            collective_id=0, has_side_effects=True, vmem_limit_bytes=48 * 1024 * 1024),
        cost_estimate=pl.CostEstimate(
            flops=6 * rows * slots * tile * width, bytes_accessed=8 * rows * width,
            transcendentals=rows * slots * tile),
    )(queries, keys, neg_mask, positive, row_weight.reshape(blocks, tile))
    return loss.reshape(rows), gq, gk


def solution(mesh):
    placed = (
        P(("dp", "rep"), None),
        P("dp", None),
        P(("dp", "rep"), None),
        P(("dp", "rep")),
        P(("dp", "rep")),
    )
    return jax.shard_map(
        body,
        mesh=mesh,
        in_specs=placed,
        out_specs=(P(("dp", "rep")), P(("dp", "rep"), None), P(("dp", "rep"), None)),
        check_vma=False,
    )
```

```python
import functools
import math

import jax
import jax.numpy as jnp
from jax import lax
from jax.experimental import pallas as pl
from jax.experimental.pallas import tpu as pltpu
from jax.sharding import PartitionSpec as P

REACH = 4
GROUP = 4
NEG = -1e30


def kernel(n, q_hbm, k_hbm, mask_hbm, pos_hbm, weight_hbm, loss, gq, gk_out,
           mask, positive, weight, q, kwin, e, coef, gk, sib, outb, inb, run_max, run_sum, pos_logit, hist,
           local_sem, g_send, g_recv, f_send, f_recv, x_send, x_recv, s_send, s_recv):
    rows, width = q.shape
    blocks, tile = weight.shape
    half = tile // 2
    scale = 2.0 / math.sqrt(width)
    d = lax.axis_index("dp")
    r = lax.axis_index("rep")
    other = 1 - r

    def dev(by):
        return lax.rem(d + by + n, n)

    r4 = lax.rem(d, GROUP)
    base = d - r4
    even = 1 - 2 * lax.rem(r4, 2)
    place = [r4, r4 + even, lax.rem(r4 + 2, GROUP), GROUP - 1 - r4]
    mate = [base + c for c in place]

    def wrap(t):
        return lax.rem(t + n, n)

    owners = mate + [wrap(d + REACH), wrap(d - REACH)] + [
        wrap(mate[k] + jnp.where(place[k] < r4, REACH, -REACH)) for k in (1, 2, 3)]

    q_copy = pltpu.make_async_copy(q_hbm, q, local_sem.at[0])
    q_copy.start()
    own = [
        pltpu.make_async_copy(k_hbm.at[pl.ds(h * half, half)], kwin.at[0, h], local_sem.at[1 + h])
        for h in range(2)
    ]
    own += [
        pltpu.make_async_copy(src, dst, local_sem.at[3 + i])
        for i, (src, dst) in enumerate(
            ((mask_hbm, mask), (pos_hbm, positive), (weight_hbm, weight)))
    ]
    for c in own:
        c.start()

    barrier = pltpu.get_barrier_semaphore()
    for to in mate[1:] + [dev(REACH), dev(-REACH)]:
        pl.semaphore_signal(barrier, inc=1, device_id={"dp": to},
                            device_id_type=pl.DeviceIdType.MESH)
    pl.semaphore_signal(barrier, inc=1, device_id={"rep": other},
                        device_id_type=pl.DeviceIdType.MESH)
    pl.semaphore_wait(barrier, GROUP + 2)

    def gather(p, to):
        return pltpu.make_async_remote_copy(
            src_ref=k_hbm.at[pl.ds(pl.multiple_of(r * half, half), half)],
            dst_ref=kwin.at[p, r],
            send_sem=g_send.at[p], recv_sem=g_recv.at[p],
            device_id={"dp": to}, device_id_type=pl.DeviceIdType.MESH)

    def relay(src, k):
        return pltpu.make_async_remote_copy(
            src_ref=kwin.at[src, r], dst_ref=kwin.at[REACH + 1 + k, r],
            send_sem=g_send.at[REACH + 1 + k], recv_sem=g_recv.at[REACH + 1 + k],
            device_id={"dp": mate[k]}, device_id_type=pl.DeviceIdType.MESH)

    def pass_on(src):
        gather(src, d).wait_recv()
        for k in (1, 2, 3):
            @pl.when(jnp.where(place[k] > r4, REACH, REACH + 1) == src)
            def _():
                relay(src, k).start()
        forward(src, r).start()

    def forward(p, h):
        return pltpu.make_async_remote_copy(
            src_ref=kwin.at[p, h], dst_ref=kwin.at[p, h],
            send_sem=f_send.at[p], recv_sem=f_recv.at[p],
            device_id={"rep": other}, device_id_type=pl.DeviceIdType.MESH)

    gather(REACH + 1, dev(REACH)).start()
    gather(REACH, dev(-REACH)).start()
    for k in (1, 2, 3):
        gather(k, mate[k]).start()

    run_max[...] = jnp.full(run_max.shape, NEG, jnp.float32)
    run_sum[...] = jnp.zeros(run_sum.shape, jnp.float32)
    pos_logit[...] = jnp.zeros(pos_logit.shape, jnp.float32)
    eye = (lax.broadcasted_iota(jnp.int32, (tile, tile), 0)
           == lax.broadcasted_iota(jnp.int32, (tile, tile), 1))
    eye_f = eye.astype(jnp.float32)

    def chunk(j, owner, first, count):
        k = kwin[pl.ds(first, count)].reshape(count * tile, width)
        group = 2 if blocks % 2 == 0 else 1
        for g in range(blocks // group):
            logit = lax.dot_general(
                k, q[g * group * tile:(g + 1) * group * tile, :],
                (((1,), (1,)), ((), ())), preferred_element_type=jnp.float32)
            for bb in range(group):
                b = g * group + bb
                lanes = slice(bb * tile, (bb + 1) * tile)
                old = run_max[b:b + 1, :]
                top = old
                masked = []
                found = pos_logit[b:b + 1, :]
                for i in range(count):
                    part = logit[i * tile:(i + 1) * tile, lanes] * scale
                    hit = positive[b] == owner[i]
                    allow = (mask[b, owner[i]] == 1) | hit
                    found = found + jnp.where(hit, 1.0, 0.0) * jnp.sum(
                        jnp.where(eye, part, 0.0), axis=0, keepdims=True)
                    part = part + jnp.where(allow, 0.0, NEG)
                    masked.append(part)
                    top = jnp.maximum(top, jnp.max(part, axis=0, keepdims=True))
                total = run_sum[b:b + 1, :] * jnp.exp(old - top)
                for i in range(count):
                    ex = jnp.exp(masked[i] - top)
                    total = total + jnp.sum(ex, axis=0, keepdims=True)
                    e[first + i, :, b * tile:(b + 1) * tile] = ex
                run_max[b:b + 1, :] = top
                run_sum[b:b + 1, :] = total
                pos_logit[b:b + 1, :] = found
        hist[j] = run_max[...]

    q_copy.wait()
    for c in own:
        c.wait()
    chunk(0, owners[:1], 0, 1)

    def pick(p):
        out = owners[-1]
        for i in range(2 * REACH):
            out = jnp.where(p == i, owners[i], out)
        return out

    near = jnp.where(d + REACH < n, REACH, REACH + 1)
    pass_on(near)

    @pl.loop(1, REACH + 1)
    def _(j):
        pair = (2 * j - 1, 2 * j)

        @pl.when(j == 2)
        def _():
            pass_on(2 * REACH + 1 - near)

        for p in pair:
            @pl.when((p != REACH) & (p != REACH + 1))
            def _():
                gather(p, d).wait_recv()
                forward(p, r).start()
        for p in pair:
            forward(p, other).wait_recv()
        chunk(j, [pick(p) for p in pair], 2 * j - 1, 2)

    log_total = run_max[...] + jnp.log(run_sum[...])
    loss[...] = log_total - pos_logit[...]
    w_over = weight[...] / run_sum[...]

    def finish(j, owner, first):
        factor = w_over * jnp.exp(hist[j] - run_max[...])
        for b in range(blocks):
            lanes = slice(b * tile, (b + 1) * tile)
            for i, o in enumerate(owner):
                at = jnp.where(positive[b] == o, 1.0, 0.0) * weight[b:b + 1, :]
                coef[first + i, :, lanes] = (
                    e[first + i, :, lanes] * factor[b:b + 1, :] - at * eye_f
                ).astype(jnp.bfloat16)

    def exchange(p, h):
        return pltpu.make_async_remote_copy(
            src_ref=gk.at[p, h], dst_ref=sib.at[p],
            send_sem=x_send.at[p], recv_sem=x_recv.at[p],
            device_id={"rep": other}, device_id_type=pl.DeviceIdType.MESH)

    def scatter(p, p_dst, to):
        return pltpu.make_async_remote_copy(
            src_ref=outb.at[p], dst_ref=inb.at[p_dst],
            send_sem=s_send.at[p], recv_sem=s_recv.at[p_dst],
            device_id={"dp": to}, device_id_type=pl.DeviceIdType.MESH)

    def key_grad(first, count):
        c = coef[pl.ds(first, count)].reshape(count * tile, rows)
        for g in range(4):
            cols = slice(g * (width // 4), (g + 1) * (width // 4))
            part = scale * jnp.dot(c, q[:, cols], preferred_element_type=jnp.float32)
            gk[pl.ds(first, count), :, :, cols] = part.reshape(count, 2, half, width // 4)

    def gather_sum(p):
        exchange(p, other).wait_recv()
        return gk[p, r] + sib[p]

    def ship(p):
        outb[p] = gather_sum(p).astype(jnp.bfloat16)
        k = jnp.where(p > REACH, p - REACH - 1, p)
        scatter(p, p, jnp.where(k == 1, mate[1], jnp.where(k == 2, mate[2], mate[3]))).start()

    @pl.loop(0, REACH)
    def _(i):
        j = REACH - i
        finish(j, [pick(2 * j - 1), pick(2 * j)], 2 * j - 1)
        key_grad(2 * j - 1, 2)
        for p in (2 * j - 1, 2 * j):
            exchange(p, other).start()
        for p in (2 * j + 1, 2 * j + 2):
            @pl.when((i > 0) & (p != REACH) & (p != REACH + 1))
            def _():
                ship(p)

    finish(0, owners[:1], 0)
    key_grad(0, 1)
    exchange(0, other).start()
    far = [gather_sum(REACH), gather_sum(REACH + 1)]
    for k in (1, 2, 3):
        scatter(REACH + 1 + k, REACH + 1 + k, d).wait_recv()
        part = inb[REACH + 1 + k].astype(jnp.float32)
        far = [far[0] + jnp.where(place[k] > r4, part, 0.0),
               far[1] + jnp.where(place[k] > r4, 0.0, part)]
    for p, p_dst, by in ((REACH, REACH + 1, REACH), (REACH + 1, REACH, -REACH)):
        outb[p] = far[p - REACH].astype(jnp.bfloat16)
        scatter(p, p_dst, dev(by)).start()
    ship(1)
    ship(2)

    k_all = kwin[...].reshape((2 * REACH + 1) * tile, width)
    c_all = coef
    step = rows // 4
    for g in range(4):
        ct = c_all[:, :, g * step:(g + 1) * step].reshape((2 * REACH + 1) * tile, step)
        gq[g * step:(g + 1) * step, :] = scale * lax.dot_general(
            ct, k_all, (((0,), (0,)), ((), ())), preferred_element_type=jnp.float32)

    exchange(0, other).wait_recv()
    acc = gk[0, r] + sib[0]
    for p in range(1, REACH + 2):
        scatter(p, p, d).wait_recv()
        acc = acc + inb[p].astype(jnp.float32)
    gk_out[...] = acc

    exchange(0, other).wait_send()
    for p in range(1, 2 * REACH + 1):
        gather(p, d).wait_send()
        forward(p, r).wait_send()
        exchange(p, other).wait_send()
        scatter(p, p, d).wait_send()


def body(queries, keys, neg_mask, positive, row_weight):
    n = lax.axis_size("dp")
    rows, width = queries.shape
    tile = keys.shape[0]
    blocks = rows // tile
    half = tile // 2
    slots = 2 * REACH + 1
    hbm, vmem, smem = (pl.BlockSpec(memory_space=m) for m in (pltpu.HBM, pltpu.VMEM, pltpu.SMEM))
    f32, bf16 = jnp.float32, jnp.bfloat16
    dma = pltpu.SemaphoreType.DMA
    loss, gq, gk = pl.pallas_call(
        functools.partial(kernel, n),
        out_shape=(
            jax.ShapeDtypeStruct((blocks, tile), f32),
            jax.ShapeDtypeStruct((rows, width), f32),
            jax.ShapeDtypeStruct((half, width), f32),
        ),
        in_specs=[hbm, hbm, hbm, hbm, hbm],
        out_specs=(vmem, vmem, vmem),
        scratch_shapes=[
            pltpu.SMEM(neg_mask.shape, jnp.int32),
            pltpu.SMEM(positive.shape, jnp.int32),
            pltpu.VMEM((blocks, tile), f32),
            pltpu.VMEM((rows, width), bf16),
            pltpu.VMEM((slots, 2, half, width), bf16),
            pltpu.VMEM((slots, tile, rows), f32),
            pltpu.VMEM((slots, tile, rows), bf16),
            pltpu.VMEM((slots, 2, half, width), f32),
            pltpu.VMEM((slots, half, width), f32),
            pltpu.VMEM((slots, half, width), bf16),
            pltpu.VMEM((slots, half, width), bf16),
            pltpu.VMEM((blocks, tile), f32),
            pltpu.VMEM((blocks, tile), f32),
            pltpu.VMEM((blocks, tile), f32),
            pltpu.VMEM((REACH + 1, blocks, tile), f32),
            dma((6,)),
            dma((slots,)), dma((slots,)), dma((slots,)), dma((slots,)),
            dma((slots,)), dma((slots,)), dma((slots,)), dma((slots,)),
        ],
        compiler_params=pltpu.CompilerParams(
            collective_id=0, has_side_effects=True, vmem_limit_bytes=40 * 1024 * 1024),
        cost_estimate=pl.CostEstimate(
            flops=6 * rows * slots * tile * width, bytes_accessed=8 * rows * width,
            transcendentals=rows * slots * tile),
    )(queries, keys, neg_mask, positive, row_weight.reshape(blocks, tile))
    return loss.reshape(rows), gq, gk


def solution(mesh):
    placed = (
        P(("dp", "rep"), None),
        P("dp", None),
        P(("dp", "rep"), None),
        P(("dp", "rep")),
        P(("dp", "rep")),
    )
    return jax.shard_map(
        body,
        mesh=mesh,
        in_specs=placed,
        out_specs=(P(("dp", "rep")), P(("dp", "rep"), None), P(("dp", "rep"), None)),
        check_vma=False,
    )
```

```python
import functools
import math

import jax
import jax.numpy as jnp
from jax import lax
from jax.experimental import pallas as pl
from jax.experimental.pallas import tpu as pltpu
from jax.sharding import PartitionSpec as P

REACH = 4
GROUP = 4
NEG = -1e30


def kernel(n, q_hbm, k_hbm, mask_hbm, pos_hbm, weight_hbm, loss, gq, gk_out,
           mask, positive, weight, q, kwin, e, coef, gk, sib, outb, inb, run_max, run_sum, pos_logit, hist,
           local_sem, g_send, g_recv, f_send, f_recv, x_send, x_recv, s_send, s_recv):
    rows, width = q.shape
    blocks, tile = weight.shape
    half = tile // 2
    scale = 2.0 / math.sqrt(width)
    d = lax.axis_index("dp")
    r = lax.axis_index("rep")
    other = 1 - r

    def dev(by):
        return lax.rem(d + by + n, n)

    r4 = lax.rem(d, GROUP)
    base = d - r4
    even = 1 - 2 * lax.rem(r4, 2)
    place = [r4, r4 + even, lax.rem(r4 + 2, GROUP), GROUP - 1 - r4]
    mate = [base + c for c in place]

    def wrap(t):
        return lax.rem(t + n, n)

    owners = mate + [wrap(d + REACH), wrap(d - REACH)] + [
        wrap(mate[k] + jnp.where(place[k] < r4, REACH, -REACH)) for k in (1, 2, 3)]

    q_copy = pltpu.make_async_copy(q_hbm, q, local_sem.at[0])
    q_copy.start()
    own = [
        pltpu.make_async_copy(k_hbm.at[pl.ds(h * half, half)], kwin.at[0, h], local_sem.at[1 + h])
        for h in range(2)
    ]
    own += [
        pltpu.make_async_copy(src, dst, local_sem.at[3 + i])
        for i, (src, dst) in enumerate(
            ((mask_hbm, mask), (pos_hbm, positive), (weight_hbm, weight)))
    ]
    for c in own:
        c.start()

    barrier = pltpu.get_barrier_semaphore()
    for to in mate[1:] + [dev(REACH), dev(-REACH)]:
        pl.semaphore_signal(barrier, inc=1, device_id={"dp": to},
                            device_id_type=pl.DeviceIdType.MESH)
    pl.semaphore_signal(barrier, inc=1, device_id={"rep": other},
                        device_id_type=pl.DeviceIdType.MESH)
    pl.semaphore_wait(barrier, GROUP + 2)

    def gather(p, to):
        return pltpu.make_async_remote_copy(
            src_ref=k_hbm.at[pl.ds(pl.multiple_of(r * half, half), half)],
            dst_ref=kwin.at[p, r],
            send_sem=g_send.at[p], recv_sem=g_recv.at[p],
            device_id={"dp": to}, device_id_type=pl.DeviceIdType.MESH)

    def relay(src, k):
        return pltpu.make_async_remote_copy(
            src_ref=kwin.at[src, r], dst_ref=kwin.at[REACH + 1 + k, r],
            send_sem=g_send.at[REACH + 1 + k], recv_sem=g_recv.at[REACH + 1 + k],
            device_id={"dp": mate[k]}, device_id_type=pl.DeviceIdType.MESH)

    def across():
        return pltpu.make_async_remote_copy(
            src_ref=kwin.at[via, r], dst_ref=kwin.at[3, r],
            send_sem=g_send.at[3], recv_sem=g_recv.at[3],
            device_id={"dp": mate_last}, device_id_type=pl.DeviceIdType.MESH)

    def pass_on(src):
        gather(src, d).wait_recv()
        for k in (1, 2, 3):
            @pl.when(jnp.where(place[k] > r4, REACH, REACH + 1) == src)
            def _():
                relay(src, k).start()
        forward(src, r).start()

    def forward(p, h):
        return pltpu.make_async_remote_copy(
            src_ref=kwin.at[p, h], dst_ref=kwin.at[p, h],
            send_sem=f_send.at[p], recv_sem=f_recv.at[p],
            device_id={"rep": other}, device_id_type=pl.DeviceIdType.MESH)

    gather(REACH + 1, dev(REACH)).start()
    gather(REACH, dev(-REACH)).start()
    via = 1 + r
    mate_via = jnp.where(via == 1, mate[1], mate[2])
    mate_last = jnp.where(via == 1, mate[2], mate[1])
    gather(via, mate_via).start()
    gather(3 - via, mate_last).start()

    run_max[...] = jnp.full(run_max.shape, NEG, jnp.float32)
    run_sum[...] = jnp.zeros(run_sum.shape, jnp.float32)
    pos_logit[...] = jnp.zeros(pos_logit.shape, jnp.float32)
    eye = (lax.broadcasted_iota(jnp.int32, (tile, tile), 0)
           == lax.broadcasted_iota(jnp.int32, (tile, tile), 1))
    eye_f = eye.astype(jnp.float32)

    def chunk(j, owner, first, count):
        k = kwin[pl.ds(first, count)].reshape(count * tile, width)
        group = 2 if blocks % 2 == 0 else 1
        for g in range(blocks // group):
            logit = lax.dot_general(
                k, q[g * group * tile:(g + 1) * group * tile, :],
                (((1,), (1,)), ((), ())), preferred_element_type=jnp.float32)
            for bb in range(group):
                b = g * group + bb
                lanes = slice(bb * tile, (bb + 1) * tile)
                old = run_max[b:b + 1, :]
                top = old
                masked = []
                found = pos_logit[b:b + 1, :]
                for i in range(count):
                    part = logit[i * tile:(i + 1) * tile, lanes] * scale
                    hit = positive[b] == owner[i]
                    allow = (mask[b, owner[i]] == 1) | hit
                    found = found + jnp.where(hit, 1.0, 0.0) * jnp.sum(
                        jnp.where(eye, part, 0.0), axis=0, keepdims=True)
                    part = part + jnp.where(allow, 0.0, NEG)
                    masked.append(part)
                    top = jnp.maximum(top, jnp.max(part, axis=0, keepdims=True))
                total = run_sum[b:b + 1, :] * jnp.exp(old - top)
                for i in range(count):
                    ex = jnp.exp(masked[i] - top)
                    total = total + jnp.sum(ex, axis=0, keepdims=True)
                    e[first + i, :, b * tile:(b + 1) * tile] = ex
                run_max[b:b + 1, :] = top
                run_sum[b:b + 1, :] = total
                pos_logit[b:b + 1, :] = found
        hist[j] = run_max[...]

    q_copy.wait()
    for c in own:
        c.wait()
    chunk(0, owners[:1], 0, 1)

    def pick(p):
        out = owners[-1]
        for i in range(2 * REACH):
            out = jnp.where(p == i, owners[i], out)
        return out

    gather(via, d).wait_recv()
    across().start()
    forward(via, r).start()
    near = jnp.where(d + REACH < n, REACH, REACH + 1)
    pass_on(near)

    @pl.loop(1, REACH + 1)
    def _(j):
        pair = (2 * j - 1, 2 * j)

        @pl.when(j == 2)
        def _():
            pass_on(2 * REACH + 1 - near)

        for p in pair:
            @pl.when((p != REACH) & (p != REACH + 1) & (p != via))
            def _():
                gather(p, d).wait_recv()
                forward(p, r).start()
        for p in pair:
            forward(p, other).wait_recv()
        chunk(j, [pick(p) for p in pair], 2 * j - 1, 2)

    log_total = run_max[...] + jnp.log(run_sum[...])
    loss[...] = log_total - pos_logit[...]
    w_over = weight[...] / run_sum[...]

    def finish(j, owner, first):
        factor = w_over * jnp.exp(hist[j] - run_max[...])
        for b in range(blocks):
            lanes = slice(b * tile, (b + 1) * tile)
            for i, o in enumerate(owner):
                at = jnp.where(positive[b] == o, 1.0, 0.0) * weight[b:b + 1, :]
                coef[first + i, :, lanes] = (
                    e[first + i, :, lanes] * factor[b:b + 1, :] - at * eye_f
                ).astype(jnp.bfloat16)

    def exchange(p, h):
        return pltpu.make_async_remote_copy(
            src_ref=gk.at[p, h], dst_ref=sib.at[p],
            send_sem=x_send.at[p], recv_sem=x_recv.at[p],
            device_id={"rep": other}, device_id_type=pl.DeviceIdType.MESH)

    def scatter(p, p_dst, to):
        return pltpu.make_async_remote_copy(
            src_ref=outb.at[p], dst_ref=inb.at[p_dst],
            send_sem=s_send.at[p], recv_sem=s_recv.at[p_dst],
            device_id={"dp": to}, device_id_type=pl.DeviceIdType.MESH)

    def key_grad(first, count):
        c = coef[pl.ds(first, count)].reshape(count * tile, rows)
        for g in range(4):
            cols = slice(g * (width // 4), (g + 1) * (width // 4))
            part = scale * jnp.dot(c, q[:, cols], preferred_element_type=jnp.float32)
            gk[pl.ds(first, count), :, :, cols] = part.reshape(count, 2, half, width // 4)

    def gather_sum(p):
        exchange(p, other).wait_recv()
        return gk[p, r] + sib[p]

    def ship(p):
        outb[p] = gather_sum(p).astype(jnp.bfloat16)
        k = jnp.where(p > REACH, p - REACH - 1, p)
        scatter(p, p, jnp.where(k == 1, mate[1], jnp.where(k == 2, mate[2], mate[3]))).start()

    @pl.loop(0, REACH)
    def _(i):
        j = REACH - i
        finish(j, [pick(2 * j - 1), pick(2 * j)], 2 * j - 1)
        key_grad(2 * j - 1, 2)
        for p in (2 * j - 1, 2 * j):
            exchange(p, other).start()
        for p in (2 * j + 1, 2 * j + 2):
            @pl.when((i > 0) & (p != REACH) & (p != REACH + 1))
            def _():
                ship(p)

    finish(0, owners[:1], 0)
    key_grad(0, 1)
    exchange(0, other).start()
    far = [gather_sum(REACH), gather_sum(REACH + 1)]
    for k in (1, 2, 3):
        scatter(REACH + 1 + k, REACH + 1 + k, d).wait_recv()
        part = inb[REACH + 1 + k].astype(jnp.float32)
        far = [far[0] + jnp.where(place[k] > r4, part, 0.0),
               far[1] + jnp.where(place[k] > r4, 0.0, part)]
    for p, p_dst, by in ((REACH, REACH + 1, REACH), (REACH + 1, REACH, -REACH)):
        outb[p] = far[p - REACH].astype(jnp.bfloat16)
        scatter(p, p_dst, dev(by)).start()
    ship(1)
    ship(2)

    k_all = kwin[...].reshape((2 * REACH + 1) * tile, width)
    c_all = coef
    step = rows // 4
    for g in range(4):
        ct = c_all[:, :, g * step:(g + 1) * step].reshape((2 * REACH + 1) * tile, step)
        gq[g * step:(g + 1) * step, :] = scale * lax.dot_general(
            ct, k_all, (((0,), (0,)), ((), ())), preferred_element_type=jnp.float32)

    exchange(0, other).wait_recv()
    acc = gk[0, r] + sib[0]
    for p in range(1, REACH + 2):
        scatter(p, p, d).wait_recv()
        acc = acc + inb[p].astype(jnp.float32)
    gk_out[...] = acc

    exchange(0, other).wait_send()
    for p in range(1, 2 * REACH + 1):
        gather(p, d).wait_send()
        forward(p, r).wait_send()
        exchange(p, other).wait_send()
        scatter(p, p, d).wait_send()


def body(queries, keys, neg_mask, positive, row_weight):
    n = lax.axis_size("dp")
    rows, width = queries.shape
    tile = keys.shape[0]
    blocks = rows // tile
    half = tile // 2
    slots = 2 * REACH + 1
    hbm, vmem, smem = (pl.BlockSpec(memory_space=m) for m in (pltpu.HBM, pltpu.VMEM, pltpu.SMEM))
    f32, bf16 = jnp.float32, jnp.bfloat16
    dma = pltpu.SemaphoreType.DMA
    loss, gq, gk = pl.pallas_call(
        functools.partial(kernel, n),
        out_shape=(
            jax.ShapeDtypeStruct((blocks, tile), f32),
            jax.ShapeDtypeStruct((rows, width), f32),
            jax.ShapeDtypeStruct((half, width), f32),
        ),
        in_specs=[hbm, hbm, hbm, hbm, hbm],
        out_specs=(vmem, vmem, vmem),
        scratch_shapes=[
            pltpu.SMEM(neg_mask.shape, jnp.int32),
            pltpu.SMEM(positive.shape, jnp.int32),
            pltpu.VMEM((blocks, tile), f32),
            pltpu.VMEM((rows, width), bf16),
            pltpu.VMEM((slots, 2, half, width), bf16),
            pltpu.VMEM((slots, tile, rows), f32),
            pltpu.VMEM((slots, tile, rows), bf16),
            pltpu.VMEM((slots, 2, half, width), f32),
            pltpu.VMEM((slots, half, width), f32),
            pltpu.VMEM((slots, half, width), bf16),
            pltpu.VMEM((slots, half, width), bf16),
            pltpu.VMEM((blocks, tile), f32),
            pltpu.VMEM((blocks, tile), f32),
            pltpu.VMEM((blocks, tile), f32),
            pltpu.VMEM((REACH + 1, blocks, tile), f32),
            dma((6,)),
            dma((slots,)), dma((slots,)), dma((slots,)), dma((slots,)),
            dma((slots,)), dma((slots,)), dma((slots,)), dma((slots,)),
        ],
        compiler_params=pltpu.CompilerParams(
            collective_id=0, has_side_effects=True, vmem_limit_bytes=40 * 1024 * 1024),
        cost_estimate=pl.CostEstimate(
            flops=6 * rows * slots * tile * width, bytes_accessed=8 * rows * width,
            transcendentals=rows * slots * tile),
    )(queries, keys, neg_mask, positive, row_weight.reshape(blocks, tile))
    return loss.reshape(rows), gq, gk


def solution(mesh):
    placed = (
        P(("dp", "rep"), None),
        P("dp", None),
        P(("dp", "rep"), None),
        P(("dp", "rep")),
        P(("dp", "rep")),
    )
    return jax.shard_map(
        body,
        mesh=mesh,
        in_specs=placed,
        out_specs=(P(("dp", "rep")), P(("dp", "rep"), None), P(("dp", "rep"), None)),
        check_vma=False,
    )
```

```python
import functools
import math

import jax
import jax.numpy as jnp
from jax import lax
from jax.experimental import pallas as pl
from jax.experimental.pallas import tpu as pltpu
from jax.sharding import PartitionSpec as P

REACH = 4
GROUP = 4
NEG = -1e30


def kernel(n, q_hbm, k_hbm, mask_hbm, pos_hbm, weight_hbm, loss, gq_hbm, gk_out,
           mask, positive, weight, q, kwin, e, coef, gk, sib, outb, inb, gq, run_max, run_sum, pos_logit, hist,
           local_sem, g_send, g_recv, f_send, f_recv, x_send, x_recv, s_send, s_recv, o_sem):
    rows, width = q.shape
    blocks, tile = weight.shape
    half = tile // 2
    scale = 2.0 / math.sqrt(width)
    d = lax.axis_index("dp")
    r = lax.axis_index("rep")
    other = 1 - r

    def dev(by):
        return lax.rem(d + by + n, n)

    r4 = lax.rem(d, GROUP)
    base = d - r4
    even = 1 - 2 * lax.rem(r4, 2)
    place = [r4, r4 + even, lax.rem(r4 + 2, GROUP), GROUP - 1 - r4]
    mate = [base + c for c in place]

    def wrap(t):
        return lax.rem(t + n, n)

    owners = mate + [wrap(d + REACH), wrap(d - REACH)] + [
        wrap(mate[k] + jnp.where(place[k] < r4, REACH, -REACH)) for k in (1, 2, 3)]

    q_copy = pltpu.make_async_copy(q_hbm, q, local_sem.at[0])
    q_copy.start()
    own = [
        pltpu.make_async_copy(k_hbm.at[pl.ds(h * half, half)], kwin.at[0, h], local_sem.at[1 + h])
        for h in range(2)
    ]
    own += [
        pltpu.make_async_copy(src, dst, local_sem.at[3 + i])
        for i, (src, dst) in enumerate(
            ((mask_hbm, mask), (pos_hbm, positive), (weight_hbm, weight)))
    ]
    for c in own:
        c.start()

    barrier = pltpu.get_barrier_semaphore()
    for to in mate[1:] + [dev(REACH), dev(-REACH)]:
        pl.semaphore_signal(barrier, inc=1, device_id={"dp": to},
                            device_id_type=pl.DeviceIdType.MESH)
    pl.semaphore_signal(barrier, inc=1, device_id={"rep": other},
                        device_id_type=pl.DeviceIdType.MESH)
    pl.semaphore_wait(barrier, GROUP + 2)

    def gather(p, to):
        return pltpu.make_async_remote_copy(
            src_ref=k_hbm.at[pl.ds(pl.multiple_of(r * half, half), half)],
            dst_ref=kwin.at[p, r],
            send_sem=g_send.at[p], recv_sem=g_recv.at[p],
            device_id={"dp": to}, device_id_type=pl.DeviceIdType.MESH)

    def relay(src, k):
        return pltpu.make_async_remote_copy(
            src_ref=kwin.at[src, r], dst_ref=kwin.at[REACH + 1 + k, r],
            send_sem=g_send.at[REACH + 1 + k], recv_sem=g_recv.at[REACH + 1 + k],
            device_id={"dp": mate[k]}, device_id_type=pl.DeviceIdType.MESH)

    def across():
        return pltpu.make_async_remote_copy(
            src_ref=kwin.at[via, r], dst_ref=kwin.at[3, r],
            send_sem=g_send.at[3], recv_sem=g_recv.at[3],
            device_id={"dp": mate_last}, device_id_type=pl.DeviceIdType.MESH)

    def pass_on(src):
        gather(src, d).wait_recv()
        for k in (1, 2, 3):
            @pl.when(jnp.where(place[k] > r4, REACH, REACH + 1) == src)
            def _():
                relay(src, k).start()
        forward(src, r).start()

    def forward(p, h):
        return pltpu.make_async_remote_copy(
            src_ref=kwin.at[p, h], dst_ref=kwin.at[p, h],
            send_sem=f_send.at[p], recv_sem=f_recv.at[p],
            device_id={"rep": other}, device_id_type=pl.DeviceIdType.MESH)

    gather(REACH + 1, dev(REACH)).start()
    gather(REACH, dev(-REACH)).start()
    via = 1 + r
    mate_via = jnp.where(via == 1, mate[1], mate[2])
    mate_last = jnp.where(via == 1, mate[2], mate[1])
    gather(via, mate_via).start()
    gather(3 - via, mate_last).start()

    run_max[...] = jnp.full(run_max.shape, NEG, jnp.float32)
    run_sum[...] = jnp.zeros(run_sum.shape, jnp.float32)
    pos_logit[...] = jnp.zeros(pos_logit.shape, jnp.float32)
    eye = (lax.broadcasted_iota(jnp.int32, (tile, tile), 0)
           == lax.broadcasted_iota(jnp.int32, (tile, tile), 1))
    eye_f = eye.astype(jnp.float32)

    def chunk(j, owner, first, count):
        k = kwin[pl.ds(first, count)].reshape(count * tile, width)
        group = 2 if blocks % 2 == 0 else 1
        for g in range(blocks // group):
            logit = lax.dot_general(
                k, q[g * group * tile:(g + 1) * group * tile, :],
                (((1,), (1,)), ((), ())), preferred_element_type=jnp.float32)
            for bb in range(group):
                b = g * group + bb
                lanes = slice(bb * tile, (bb + 1) * tile)
                old = run_max[b:b + 1, :]
                top = old
                masked = []
                found = pos_logit[b:b + 1, :]
                for i in range(count):
                    part = logit[i * tile:(i + 1) * tile, lanes] * scale
                    hit = positive[b] == owner[i]
                    allow = (mask[b, owner[i]] == 1) | hit
                    found = found + jnp.where(hit, 1.0, 0.0) * jnp.sum(
                        jnp.where(eye, part, 0.0), axis=0, keepdims=True)
                    part = part + jnp.where(allow, 0.0, NEG)
                    masked.append(part)
                    top = jnp.maximum(top, jnp.max(part, axis=0, keepdims=True))
                total = run_sum[b:b + 1, :] * jnp.exp(old - top)
                for i in range(count):
                    ex = jnp.exp(masked[i] - top)
                    total = total + jnp.sum(ex, axis=0, keepdims=True)
                    e[first + i, :, b * tile:(b + 1) * tile] = ex
                run_max[b:b + 1, :] = top
                run_sum[b:b + 1, :] = total
                pos_logit[b:b + 1, :] = found
        hist[j] = run_max[...]

    q_copy.wait()
    for c in own:
        c.wait()
    chunk(0, owners[:1], 0, 1)

    def pick(p):
        out = owners[-1]
        for i in range(2 * REACH):
            out = jnp.where(p == i, owners[i], out)
        return out

    gather(via, d).wait_recv()
    across().start()
    forward(via, r).start()
    near = jnp.where(d + REACH < n, REACH, REACH + 1)
    pass_on(near)

    @pl.loop(1, REACH + 1)
    def _(j):
        pair = (2 * j - 1, 2 * j)

        @pl.when(j == 2)
        def _():
            pass_on(2 * REACH + 1 - near)

        for p in pair:
            @pl.when((p != REACH) & (p != REACH + 1) & (p != via))
            def _():
                gather(p, d).wait_recv()
                forward(p, r).start()
        for p in pair:
            forward(p, other).wait_recv()
        chunk(j, [pick(p) for p in pair], 2 * j - 1, 2)

    log_total = run_max[...] + jnp.log(run_sum[...])
    loss[...] = log_total - pos_logit[...]
    w_over = weight[...] / run_sum[...]

    def finish(j, owner, first):
        factor = w_over * jnp.exp(hist[j] - run_max[...])
        for b in range(blocks):
            lanes = slice(b * tile, (b + 1) * tile)
            for i, o in enumerate(owner):
                at = jnp.where(positive[b] == o, 1.0, 0.0) * weight[b:b + 1, :]
                coef[first + i, :, lanes] = (
                    e[first + i, :, lanes] * factor[b:b + 1, :] - at * eye_f
                ).astype(jnp.bfloat16)

    def exchange(p, h):
        return pltpu.make_async_remote_copy(
            src_ref=gk.at[p, h], dst_ref=sib.at[p],
            send_sem=x_send.at[p], recv_sem=x_recv.at[p],
            device_id={"rep": other}, device_id_type=pl.DeviceIdType.MESH)

    def scatter(p, p_dst, to):
        return pltpu.make_async_remote_copy(
            src_ref=outb.at[p], dst_ref=inb.at[p_dst],
            send_sem=s_send.at[p], recv_sem=s_recv.at[p_dst],
            device_id={"dp": to}, device_id_type=pl.DeviceIdType.MESH)

    def key_grad(first, count):
        c = coef[pl.ds(first, count)].reshape(count * tile, rows)
        for g in range(4):
            cols = slice(g * (width // 4), (g + 1) * (width // 4))
            part = scale * jnp.dot(c, q[:, cols], preferred_element_type=jnp.float32)
            gk[pl.ds(first, count), :, :, cols] = part.reshape(count, 2, half, width // 4)

    def gather_sum(p):
        exchange(p, other).wait_recv()
        return gk[p, r] + sib[p]

    def ship(p):
        outb[p] = gather_sum(p).astype(jnp.bfloat16)
        k = jnp.where(p > REACH, p - REACH - 1, p)
        scatter(p, p, jnp.where(k == 1, mate[1], jnp.where(k == 2, mate[2], mate[3]))).start()

    @pl.loop(0, REACH)
    def _(i):
        j = REACH - i
        finish(j, [pick(2 * j - 1), pick(2 * j)], 2 * j - 1)
        key_grad(2 * j - 1, 2)
        for p in (2 * j - 1, 2 * j):
            exchange(p, other).start()
        for p in (2 * j + 1, 2 * j + 2):
            @pl.when((i > 0) & (p != REACH) & (p != REACH + 1))
            def _():
                ship(p)

    finish(0, owners[:1], 0)
    key_grad(0, 1)
    exchange(0, other).start()
    far = [gather_sum(REACH), gather_sum(REACH + 1)]
    for k in (1, 2, 3):
        scatter(REACH + 1 + k, REACH + 1 + k, d).wait_recv()
        part = inb[REACH + 1 + k].astype(jnp.float32)
        far = [far[0] + jnp.where(place[k] > r4, part, 0.0),
               far[1] + jnp.where(place[k] > r4, 0.0, part)]
    for p, p_dst, by in ((REACH, REACH + 1, REACH), (REACH + 1, REACH, -REACH)):
        outb[p] = far[p - REACH].astype(jnp.bfloat16)
        scatter(p, p_dst, dev(by)).start()
    ship(1)
    ship(2)

    def give(g):
        part = pl.ds(g * (rows // 4), rows // 4)
        return pltpu.make_async_copy(gq.at[part], gq_hbm.at[part], o_sem.at[g])

    k_all = kwin[...].reshape((2 * REACH + 1) * tile, width)
    c_all = coef
    step = rows // 4
    for g in range(4):
        ct = c_all[:, :, g * step:(g + 1) * step].reshape((2 * REACH + 1) * tile, step)
        gq[g * step:(g + 1) * step, :] = scale * lax.dot_general(
            ct, k_all, (((0,), (0,)), ((), ())), preferred_element_type=jnp.float32)
        give(g).start()

    exchange(0, other).wait_recv()
    acc = gk[0, r] + sib[0]
    for p in range(1, REACH + 2):
        scatter(p, p, d).wait_recv()
        acc = acc + inb[p].astype(jnp.float32)
    gk_out[...] = acc
    for g in range(4):
        give(g).wait()

    exchange(0, other).wait_send()
    for p in range(1, 2 * REACH + 1):
        gather(p, d).wait_send()
        forward(p, r).wait_send()
        exchange(p, other).wait_send()
        scatter(p, p, d).wait_send()


def body(queries, keys, neg_mask, positive, row_weight):
    n = lax.axis_size("dp")
    rows, width = queries.shape
    tile = keys.shape[0]
    blocks = rows // tile
    half = tile // 2
    slots = 2 * REACH + 1
    hbm, vmem, smem = (pl.BlockSpec(memory_space=m) for m in (pltpu.HBM, pltpu.VMEM, pltpu.SMEM))
    f32, bf16 = jnp.float32, jnp.bfloat16
    dma = pltpu.SemaphoreType.DMA
    loss, gq, gk = pl.pallas_call(
        functools.partial(kernel, n),
        out_shape=(
            jax.ShapeDtypeStruct((blocks, tile), f32),
            jax.ShapeDtypeStruct((rows, width), f32),
            jax.ShapeDtypeStruct((half, width), f32),
        ),
        in_specs=[hbm, hbm, hbm, hbm, hbm],
        out_specs=(vmem, hbm, vmem),
        scratch_shapes=[
            pltpu.SMEM(neg_mask.shape, jnp.int32),
            pltpu.SMEM(positive.shape, jnp.int32),
            pltpu.VMEM((blocks, tile), f32),
            pltpu.VMEM((rows, width), bf16),
            pltpu.VMEM((slots, 2, half, width), bf16),
            pltpu.VMEM((slots, tile, rows), f32),
            pltpu.VMEM((slots, tile, rows), bf16),
            pltpu.VMEM((slots, 2, half, width), f32),
            pltpu.VMEM((slots, half, width), f32),
            pltpu.VMEM((slots, half, width), bf16),
            pltpu.VMEM((slots, half, width), bf16),
            pltpu.VMEM((rows, width), f32),
            pltpu.VMEM((blocks, tile), f32),
            pltpu.VMEM((blocks, tile), f32),
            pltpu.VMEM((blocks, tile), f32),
            pltpu.VMEM((REACH + 1, blocks, tile), f32),
            dma((6,)),
            dma((slots,)), dma((slots,)), dma((slots,)), dma((slots,)),
            dma((slots,)), dma((slots,)), dma((slots,)), dma((slots,)),
            dma((4,)),
        ],
        compiler_params=pltpu.CompilerParams(
            collective_id=0, has_side_effects=True, vmem_limit_bytes=58 * 1024 * 1024),
        cost_estimate=pl.CostEstimate(
            flops=6 * rows * slots * tile * width, bytes_accessed=8 * rows * width,
            transcendentals=rows * slots * tile),
    )(queries, keys, neg_mask, positive, row_weight.reshape(blocks, tile))
    return loss.reshape(rows), gq, gk


def solution(mesh):
    placed = (
        P(("dp", "rep"), None),
        P("dp", None),
        P(("dp", "rep"), None),
        P(("dp", "rep")),
        P(("dp", "rep")),
    )
    return jax.shard_map(
        body,
        mesh=mesh,
        in_specs=placed,
        out_specs=(P(("dp", "rep")), P(("dp", "rep"), None), P(("dp", "rep"), None)),
        check_vma=False,
    )
```
